32 devices in a mesh: lat: 16 (over z, y, x), grow: 2 (over core).
Axes of the slice: x: 2, y: 2, z: 4, core: 2. Of those that a mesh axis runs over, the one named last changes fastest.
Arguments:
- phase: float32 [32, 64, 1536], P('grow', 'lat'), may hold values from -1 to 1
- solute: float32 [32, 64, 1536], P('grow', 'lat'), may hold values from -3 to 3
- seed_grain: int32 [1536], replicated, may hold values 0 or 1
- writer: int32 [2, 16], replicated, may hold values from 0 to 15, each once within a row
Outputs:
- phase_out: float32 [32, 64, 1536], P('grow', 'lat')
- solute_out: float32 [32, 64, 1536], P('grow', 'lat')
- checkpoint: float32 [2, 16, 2, 4, 1, 192], P('grow', 'lat')
The draws below stay inside these ranges and needn't reach their ends.
Inputs may be any that keep to these rules, and one draw needn't show every extreme that they name: Each row of writer is a permutation of 0 to 15.
All inputs are finite; a program needn't handle non-finite values.
Results may differ from the reference program's by a relative error of at most 0.0003.
Values sent between devices are 32-bit elements; how exact they have to be, the bound alone decides.
A program may use at most 64 MiB of HBM per device.

```python
import jax
import jax.numpy as jnp
from jax import lax

CX = 4
NY = 1536
SHIFT = 16
NX = 64
NZ = 32
WRITERS = 16
GROUPS = 2


def place_ends(values, rng, least, largest):
    longest = values.shape.index(max(values.shape))
    spots = []
    for shift in (0, 1):
        where = [jax.random.randint(jax.random.fold_in(rng, axis), (), 0, length) for axis, length in enumerate(values.shape)]
        where[longest] = (where[longest] + shift) % values.shape[longest]
        spots.append(tuple(where))
    return values.at[spots[0]].set(least).at[spots[1]].set(largest)


def shard_levels(stream_key, extent, shards, smallest, top_value):
    level = 1.0
    for axis_at, shards_of in shards:
        draws = jax.random.uniform(jax.random.fold_in(jax.random.fold_in(stream_key, 6), axis_at), (shards_of,), jnp.float32, smallest / len(shards), top_value / len(shards))
        level = level * jnp.repeat(jnp.exp(draws), extent[axis_at] // shards_of).reshape((-1,) + (1,) * (len(extent) - 1 - axis_at))
    return level


def bell_draw(stream_key, dims, spread, bound, cuts=(), held_as=jnp.bfloat16):
    gain = shard_levels(stream_key, dims, cuts, -0.22, 0.18) if cuts else 1.0
    entries = jax.random.normal(stream_key, dims, jnp.float32) * spread * gain
    return jnp.minimum(jnp.maximum(entries, -bound), bound).astype(held_as)


def setup_inputs(seed: int = 0) -> dict:
    splits = jax.random.split(jax.random.key(seed), 5)
    phase = jnp.clip(jax.random.uniform(splits[0], (NZ, NX, NY), jnp.float32, -1.0, 1.0) * shard_levels(splits[0], (NZ, NX, NY), ((0, 2), (1, 16)), -0.4, 0.0), -1.0, 1.0)
    solute = bell_draw(splits[1], (NZ, NX, NY), 0.5, 3.0, ((0, 2), (1, 16)), jnp.float32)
    seed_grain = place_ends((jax.random.randint(splits[2], (NY,), 0, 2) < 1).astype(jnp.int32), jax.random.fold_in(splits[2], 1), 0, 1)
    writer = jax.vmap(lambda own: jax.random.permutation(own, WRITERS))(jax.random.split(splits[3], GROUPS)).reshape((GROUPS, WRITERS)).astype(jnp.int32)
    return dict(phase=phase, solute=solute, seed_grain=seed_grain, writer=writer)


time_step = 0.15
aniso_strength = 0.15
coupling = 3.0
partition = 0.15
grad_floor = 0.25
solid_u = -0.5
liquid_u = 0.0
half_root = 0.7071067811865476


def advance(ext, grain, theta):
    phi_e = ext[0]
    sol_e = ext[1]
    p = phi_e[1:-1, 1:-1]
    pzp = phi_e[2:, 1:-1]
    pzm = phi_e[:-2, 1:-1]
    pxp = phi_e[1:-1, 2:]
    pxm = phi_e[1:-1, :-2]
    pyp = jnp.roll(p, -1, 2)
    pym = jnp.roll(p, 1, 2)
    grad_z = 0.5 * (pzp - pzm)
    grad_x = 0.5 * (pxp - pxm)
    grad_y = 0.5 * (pyp - pym)
    turned_x = (grad_x + grad_y) * half_root
    turned_y = (grad_x - grad_y) * half_root
    comp_x = jnp.where(grain, turned_x, grad_x)
    comp_y = jnp.where(grain, turned_y, grad_y)
    sq_x = comp_x * comp_x
    sq_y = comp_y * comp_y
    sq_z = grad_z * grad_z
    total_sq = sq_x + sq_y + sq_z
    quartic = sq_x * sq_x + sq_y * sq_y + sq_z * sq_z
    floored = jnp.maximum(total_sq, grad_floor)
    aniso = 1.0 + aniso_strength * (4.0 * quartic / (floored * floored) - 3.0)
    aniso_sq = aniso * aniso
    laplace = pzp + pzm + pxp + pxm + pyp + pym - 6.0 * p
    u = sol_e[1:-1, 1:-1]
    drive = p - p * p * p - coupling * (1.0 - p * p) ** 2 * (u + theta[:, None, None])
    rate = (aniso_sq * laplace + drive) / aniso_sq
    q_e = 0.5 * (1.0 - jnp.clip(phi_e, -1.0, 1.0))
    q = q_e[1:-1, 1:-1]
    uzp = sol_e[2:, 1:-1]
    uzm = sol_e[:-2, 1:-1]
    uxp = sol_e[1:-1, 2:]
    uxm = sol_e[1:-1, :-2]
    uyp = jnp.roll(u, -1, 2)
    uym = jnp.roll(u, 1, 2)
    flux = 0.5 * (q + q_e[2:, 1:-1]) * (uzp - u)
    flux = flux + 0.5 * (q + q_e[:-2, 1:-1]) * (uzm - u)
    flux = flux + 0.5 * (q + q_e[1:-1, 2:]) * (uxp - u)
    flux = flux + 0.5 * (q + q_e[1:-1, :-2]) * (uxm - u)
    flux = flux + 0.5 * (q + jnp.roll(q, -1, 2)) * (uyp - u)
    flux = flux + 0.5 * (q + jnp.roll(q, 1, 2)) * (uym - u)
    weight = 0.5 * (1.0 + partition - (1.0 - partition) * jnp.clip(p, -1.0, 1.0))
    urate = (flux + 0.5 * (1.0 + (1.0 - partition) * u) * rate) / weight
    return jnp.stack([p + time_step * rate, u + time_step * urate])


def full_step(state, grain, theta):
    wide = jnp.concatenate([state[:, :, -1:], state, state[:, :, :1]], axis=2)
    shape_plane = (1, 1, wide.shape[2], wide.shape[3])
    bottom = jnp.concatenate([jnp.full(shape_plane, 1.0, jnp.float32), jnp.full(shape_plane, solid_u, jnp.float32)], axis=0)
    top = jnp.concatenate([jnp.full(shape_plane, -1.0, jnp.float32), jnp.full(shape_plane, liquid_u, jnp.float32)], axis=0)
    padded = jnp.concatenate([bottom, wide, top], axis=1)
    block = 8
    count = state.shape[1] // block

    def one_block(index):
        start = (index * block).astype(jnp.int32)
        ext = lax.dynamic_slice_in_dim(padded, start, block + 2, axis=1)
        local_theta = lax.dynamic_slice_in_dim(theta, start, block, axis=0)
        return advance(ext, grain, local_theta)

    pieces = lax.map(one_block, jnp.arange(count, dtype=jnp.int32))
    pieces = jnp.moveaxis(pieces, 0, 1)
    return pieces.reshape(state.shape)


def reference(phase, solute, seed_grain, writer):
    grain = seed_grain > 0
    state = jnp.stack([phase, solute])
    theta = (jnp.arange(NZ).astype(jnp.float32) + 0.5) / NZ - 0.5
    for turn in range(2):
        state = full_step(state, grain, theta)
    lower = state[:, :SHIFT]
    coarse = lower.reshape(2, SHIFT // 4, 4, NX // 4, 4, NY // 4, 4).mean(axis=(2, 4, 6))
    fill = jnp.concatenate([jnp.full((1, SHIFT, NX, NY), -1.0, jnp.float32), jnp.full((1, SHIFT, NX, NY), liquid_u, jnp.float32)], axis=0)
    moved = jnp.concatenate([state[:, SHIFT:], fill], axis=1)
    piece = NY // (4 * GROUPS)
    blocks = coarse.reshape(2, SHIFT // 4, WRITERS, CX // 4, GROUPS, piece)
    blocks = jnp.transpose(blocks, (4, 2, 0, 1, 3, 5))
    rows = jnp.arange(GROUPS).astype(jnp.int32)[:, None] + jnp.zeros((GROUPS, WRITERS), jnp.int32)
    checkpoint = jnp.zeros(blocks.shape, jnp.float32).at[rows, writer].set(blocks)
    return moved[0], moved[1], checkpoint
```

```python
import functools

import jax
import jax.numpy as jnp
from jax import lax
from jax.experimental import pallas as pl
from jax.experimental.pallas import tpu as pltpu
from jax.sharding import PartitionSpec as P

time_step = 0.15
aniso_strength = 0.15
coupling = 3.0
partition = 0.15
grad_floor = 0.25
solid_u = -0.5
liquid_u = 0.0
half_root = 0.7071067811865476
MESH = pl.DeviceIdType.MESH


def clip(v):
    return jnp.minimum(jnp.maximum(v, -1.0), 1.0)


def advance(fields, index, grain, theta):
    p = fields[0, index]
    u = fields[1, index]
    pzp = fields[0, index + 1]
    pzm = fields[0, index - 1]
    uzp = fields[1, index + 1]
    uzm = fields[1, index - 1]
    rows, width = p.shape

    def around(v):
        return (
            pltpu.roll(v, rows - 1, 0),
            pltpu.roll(v, 1, 0),
            pltpu.roll(v, width - 1, 1),
            pltpu.roll(v, 1, 1),
        )

    pxp, pxm, pyp, pym = around(p)
    grad_z = 0.5 * (pzp - pzm)
    grad_x = 0.5 * (pxp - pxm)
    grad_y = 0.5 * (pyp - pym)
    turned_x = (grad_x + grad_y) * half_root
    turned_y = (grad_x - grad_y) * half_root
    comp_x = jnp.where(grain, turned_x, grad_x)
    comp_y = jnp.where(grain, turned_y, grad_y)
    sq_x = comp_x * comp_x
    sq_y = comp_y * comp_y
    sq_z = grad_z * grad_z
    total_sq = sq_x + sq_y + sq_z
    quartic = sq_x * sq_x + sq_y * sq_y + sq_z * sq_z
    floored = jnp.maximum(total_sq, grad_floor)
    aniso = 1.0 + aniso_strength * (4.0 * quartic / (floored * floored) - 3.0)
    aniso_sq = aniso * aniso
    laplace = pzp + pzm + pxp + pxm + pyp + pym - 6.0 * p
    left = 1.0 - p * p
    drive = p - p * p * p - coupling * (left * left) * (u + theta)
    rate = laplace + drive / aniso_sq
    clipped = clip(p)
    base = 2.0 - clipped
    flux = (base - clip(pzp)) * (uzp - u) + (base - clip(pzm)) * (uzm - u)
    for pn, un in zip((pxp, pxm, pyp, pym), around(u)):
        flux = flux + (base - clip(pn)) * (un - u)
    weight = 0.5 * (1.0 + partition - (1.0 - partition) * clipped)
    urate = (0.25 * flux + 0.5 * (1.0 + (1.0 - partition) * u) * rate) / weight
    return p + time_step * rate, u + time_step * urate


def kernel(
    lat_count, grow_count, phase, solute, grain_ref, writer,
    phase_out, solute_out, check_out,
    to_left, to_right, from_left, from_right, ext, mid, fin, pieces, landed,
    left_send, right_send, left_recv, right_recv, z_send, z_recv, out_send, out_recv,
    piece_send, piece_recv,
):
    planes, rows, width = phase.shape
    lat = lax.axis_index("lat")
    grow = lax.axis_index("grow")
    left = lax.rem(lat + lat_count - 1, lat_count)
    right = lax.rem(lat + 1, lat_count)
    top = grow == grow_count - 1
    bottom = grow == 0
    total = planes * grow_count
    pairs = planes // 2

    barrier = pltpu.get_barrier_semaphore()

    def greet(a, b):
        pl.semaphore_signal(barrier, inc=1, device_id=(a, b), device_id_type=MESH)

    @pl.when(bottom)
    def _():
        def one(k, carry):
            peer = lax.rem(lat + k, lat_count)
            for r in range(grow_count):
                if r == 0:
                    @pl.when(k > 0)
                    def _():
                        greet(peer, r)
                else:
                    greet(peer, r)
            return carry
        lax.fori_loop(0, lat_count, one, 0)

    @pl.when(grow > 0)
    def _():
        def one(k, carry):
            greet(lax.rem(lat + k, lat_count), 0)
            return carry
        lax.fori_loop(0, lat_count, one, 0)
        greet(left, grow)
        greet(right, grow)

        @pl.when(grow > 1)
        def _():
            greet(lat, grow - 1)

        @pl.when(grow < grow_count - 1)
        def _():
            greet(lat, grow + 1)

    def pack(z, carry):
        to_right[z, 0:2, :] = phase[z, rows - 2 : rows, :]
        to_right[z, 2:4, :] = solute[z, rows - 2 : rows, :]
        to_left[z, 0:2, :] = phase[z, 0:2, :]
        to_left[z, 2:4, :] = solute[z, 0:2, :]
        return carry

    lax.fori_loop(0, planes, pack, 0)

    @pl.when(bottom)
    def _():
        pl.semaphore_wait(barrier, lat_count * grow_count - 1)

    @pl.when(grow > 0)
    def _():
        pl.semaphore_wait(barrier, lat_count + 2)

        @pl.when(grow > 1)
        def _():
            pl.semaphore_wait(barrier, 1)

        @pl.when(grow < grow_count - 1)
        def _():
            pl.semaphore_wait(barrier, 1)

    def sides(chunk):
        part = pl.ds(2 * chunk, 2)
        return (
            pltpu.make_async_remote_copy(
                src_ref=to_right.at[part], dst_ref=from_left.at[part],
                send_sem=right_send.at[chunk], recv_sem=left_recv.at[chunk],
                device_id=(right, grow), device_id_type=MESH),
            pltpu.make_async_remote_copy(
                src_ref=to_left.at[part], dst_ref=from_right.at[part],
                send_sem=left_send.at[chunk], recv_sem=right_recv.at[chunk],
                device_id=(left, grow), device_id_type=MESH),
        )

    def begin(k, carry):
        for copy in sides(lax.rem(k + pairs - 1, pairs)):
            copy.start()
        return carry

    lax.fori_loop(0, pairs, begin, 0)

    def own(z, carry):
        ext[0, z + 2, 2 : 2 + rows, :] = phase[z]
        ext[1, z + 2, 2 : 2 + rows, :] = solute[z]
        return carry

    lax.fori_loop(0, planes, own, 0)

    grain = grain_ref[...] > 0
    grain = jnp.broadcast_to(grain, (rows + 4, width))

    def up_copy():
        return pltpu.make_async_remote_copy(
            src_ref=ext.at[:, pl.ds(planes, 2)], dst_ref=ext.at[:, pl.ds(0, 2)],
            send_sem=z_send.at[0], recv_sem=z_recv.at[0],
            device_id=(lat, jnp.minimum(grow + 1, grow_count - 1)), device_id_type=MESH)

    def down_copy():
        return pltpu.make_async_remote_copy(
            src_ref=ext.at[:, pl.ds(2, 2)], dst_ref=ext.at[:, pl.ds(planes + 2, 2)],
            send_sem=z_send.at[1], recv_sem=z_recv.at[1],
            device_id=(lat, jnp.maximum(grow - 1, 0)), device_id_type=MESH)

    def out_copies(pair):
        part = pl.ds(2 * pair, 2)
        return [
            pltpu.make_async_remote_copy(
                src_ref=fin.at[f, part], dst_ref=(phase_out, solute_out)[f].at[part],
                send_sem=out_send.at[f, pair], recv_sem=out_recv.at[f, pair],
                device_id=(lat, jnp.maximum(grow - 1, 0)), device_id_type=MESH)
            for f in range(2)
        ]

    def level(z):
        return ((grow * planes + z).astype(jnp.float32) + 0.5) / total - 0.5

    def first(j, carry):
        e = lax.rem(j + planes, planes + 2) + 1
        new_p, new_u = advance(ext, e, grain, level(e - 2))
        mid[0, e - 1] = new_p
        mid[1, e - 1] = new_u
        return carry

    def second(pair, carry):
        def plane(z, inner):
            new_p, new_u = advance(mid, z + 1, grain, level(z))
            fin[0, z] = new_p[2 : 2 + rows]
            fin[1, z] = new_u[2 : 2 + rows]
            return inner
        lax.fori_loop(2 * pair, 2 * pair + 2, plane, 0)

        @pl.when(grow > 0)
        def _():
            for copy in out_copies(pair):
                copy.start()
        return carry

    def fill(target, start, count, values):
        for f in range(2):
            target[f, start : start + count] = jnp.full(
                (count,) + target.shape[2:], values[f], jnp.float32)

    def turn(i, carry):
        chunk = lax.rem(i + pairs - 1, pairs)
        for copy in sides(chunk):
            copy.wait_recv()
        for k in range(2):
            z = 2 * chunk + k
            for f in range(2):
                ext[f, z + 2, 0:2, :] = from_left[z, 2 * f : 2 * f + 2, :]
                ext[f, z + 2, 2 + rows : 4 + rows, :] = from_right[z, 2 * f : 2 * f + 2, :]

        @pl.when((i == 0) & jnp.logical_not(top))
        def _():
            up_copy().start()

        @pl.when(i == 1)
        def _():
            @pl.when(grow > 0)
            def _():
                down_copy().start()

            @pl.when(bottom)
            def _():
                fill(ext, 0, 2, (1.0, solid_u))

            @pl.when(top)
            def _():
                fill(ext, planes + 2, 2, (-1.0, liquid_u))

            @pl.when(grow > 0)
            def _():
                up_copy().wait_recv()

            @pl.when(jnp.logical_not(top))
            def _():
                down_copy().wait_recv()

        low = jnp.where(i <= 1, 0, 2 * i)
        high = jnp.where(i == 0, 0, jnp.where(i == pairs - 1, planes + 2, 2 * i + 2))
        lax.fori_loop(low, high, first, 0)

        @pl.when(i == 1)
        def _():
            @pl.when(bottom)
            def _():
                fill(mid, 0, 1, (1.0, solid_u))

            @pl.when(top)
            def _():
                fill(mid, planes + 1, 1, (-1.0, liquid_u))

        low = jnp.maximum(i - 2, 0)
        high = jnp.where(i == pairs - 1, pairs, jnp.maximum(i - 1, 0))
        lax.fori_loop(low, high, second, 0)
        return carry

    lax.fori_loop(0, pairs, turn, 0)

    @pl.when(top)
    def _():
        phase_out[...] = jnp.full(phase_out.shape, -1.0, jnp.float32)
        solute_out[...] = jnp.full(solute_out.shape, liquid_u, jnp.float32)

    span = width // grow_count
    lanes = pieces.shape[2]

    @pl.when(bottom)
    def _():
        sums = []
        for f in range(2):
            for group in range(planes // 4):
                four = fin[f, 4 * group] + fin[f, 4 * group + 1]
                four = four + fin[f, 4 * group + 2] + fin[f, 4 * group + 3]
                sums.append(jnp.sum(four, axis=0, keepdims=True))
        sums = jnp.concatenate(sums, axis=0) * (1.0 / 64.0)
        cell = lax.broadcasted_iota(jnp.int32, (span, lanes), 0)
        lane = lax.broadcasted_iota(jnp.int32, (span, lanes), 1)
        pick = jnp.where((cell >= 4 * lane) & (cell < 4 * lane + 4), 1.0, 0.0).astype(jnp.bfloat16)
        high = sums.astype(jnp.bfloat16).astype(jnp.float32)
        rest = sums - high
        middle = rest.astype(jnp.bfloat16).astype(jnp.float32)
        low = rest - middle
        count = sums.shape[0]
        parts = jnp.concatenate([high, middle, low, jnp.zeros_like(low)], axis=0).astype(jnp.bfloat16)
        for r in range(grow_count):
            out = jnp.dot(parts[:, r * span : (r + 1) * span], pick, preferred_element_type=jnp.float32)
            pieces[r] = out[0:count] + out[count : 2 * count] + out[2 * count : 3 * count]
        landed[lat] = pieces[0]

        def send(k, carry):
            peer = lax.rem(lat + k, lat_count)
            for r in range(grow_count):
                def go(r=r):
                    pltpu.make_async_remote_copy(
                        src_ref=pieces.at[r], dst_ref=landed.at[lat],
                        send_sem=piece_send.at[r], recv_sem=piece_recv,
                        device_id=(peer, r), device_id_type=MESH).start()
                if r == 0:
                    pl.when(k > 0)(go)
                else:
                    go()
            return carry
        lax.fori_loop(0, lat_count, send, 0)

    def finish(k, carry):
        for copy in sides(k):
            copy.wait_send()

        @pl.when(grow > 0)
        def _():
            for copy in out_copies(k):
                copy.wait_send()

        @pl.when(jnp.logical_not(top))
        def _():
            for copy in out_copies(k):
                copy.wait_recv()
        return carry

    lax.fori_loop(0, pairs, finish, 0)

    @pl.when(jnp.logical_not(top))
    def _():
        up_copy().wait_send()

    @pl.when(grow > 0)
    def _():
        down_copy().wait_send()

    others = landed.at[pl.ds(0, lat_count - 1)]

    @pl.when(bottom)
    def _():
        pltpu.make_async_copy(others, others, piece_recv).wait()

    @pl.when(grow > 0)
    def _():
        pltpu.make_async_copy(landed, landed, piece_recv).wait()

    def find(k, found):
        return jnp.where(writer[grow, k] == lat, k, found)

    mine = landed[lax.fori_loop(0, lat_count, find, 0)]
    for f in range(2):
        for group in range(planes // 4):
            at = f * (planes // 4) + group
            check_out[0, 0, f, group] = mine[at : at + 1, 0 : check_out.shape[5]]

    @pl.when(bottom)
    def _():
        pltpu.make_async_copy(others, others, piece_send.at[0]).wait()
        for r in range(1, grow_count):
            pltpu.make_async_copy(landed, landed, piece_send.at[r]).wait()


def shards(phase, solute, seed_grain, writer):
    planes, rows, width = phase.shape
    lat_count = lax.axis_size("lat")
    grow_count = lax.axis_size("grow")
    piece = width // 4 // grow_count
    lanes = -(-piece // 128) * 128
    wide = rows + 4
    pairs = planes // 2
    f32 = jnp.float32
    dma = pltpu.SemaphoreType.DMA
    vmem = pl.BlockSpec(memory_space=pltpu.VMEM)
    return tuple(pl.pallas_call(
        functools.partial(kernel, lat_count, grow_count),
        out_shape=(
            jax.ShapeDtypeStruct(phase.shape, f32),
            jax.ShapeDtypeStruct(phase.shape, f32),
            jax.ShapeDtypeStruct((1, 1, 2, planes // 4, rows // 4, piece), f32),
        ),
        in_specs=[vmem, vmem, vmem, pl.BlockSpec(memory_space=pltpu.SMEM)],
        out_specs=(vmem, vmem, vmem),
        scratch_shapes=[
            pltpu.VMEM((planes, 4, width), f32),
            pltpu.VMEM((planes, 4, width), f32),
            pltpu.VMEM((planes, 4, width), f32),
            pltpu.VMEM((planes, 4, width), f32),
            pltpu.VMEM((2, planes + 4, wide, width), f32),
            pltpu.VMEM((2, planes + 2, wide, width), f32),
            pltpu.VMEM((2, planes, rows, width), f32),
            pltpu.VMEM((grow_count, planes // 2, lanes), f32),
            pltpu.VMEM((lat_count, planes // 2, lanes), f32),
            dma((pairs,)), dma((pairs,)), dma((pairs,)), dma((pairs,)),
            dma((2,)), dma((2,)), dma((2, pairs)), dma((2, pairs)),
            dma((grow_count,)), dma,
        ],
        compiler_params=pltpu.CompilerParams(
            collective_id=0, has_side_effects=True, vmem_limit_bytes=48 * 1024 * 1024),
    )(phase, solute, seed_grain.reshape(1, width), writer))


def solution(mesh):
    placed = (P("grow", "lat", None), P("grow", "lat", None), P(), P())
    return jax.shard_map(
        shards,
        mesh=mesh,
        in_specs=placed,
        out_specs=(
            P("grow", "lat", None),
            P("grow", "lat", None),
            P("grow", "lat", None, None, None, None),
        ),
        check_vma=False,
    )
```

```python
import functools

import jax
import jax.numpy as jnp
from jax import lax
from jax.experimental import pallas as pl
from jax.experimental.pallas import tpu as pltpu
from jax.sharding import PartitionSpec as P

time_step = 0.15
aniso_strength = 0.15
coupling = 3.0
partition = 0.15
grad_floor = 0.25
solid_u = -0.5
liquid_u = 0.0
half_root = 0.7071067811865476
MESH = pl.DeviceIdType.MESH
vmem_bytes = 62 * 1024 * 1024


def clip(v):
    return jnp.minimum(jnp.maximum(v, -1.0), 1.0)


def advance(fields, index, grain, theta):
    p = fields[0, index]
    u = fields[1, index]
    pzp = fields[0, index + 1]
    pzm = fields[0, index - 1]
    uzp = fields[1, index + 1]
    uzm = fields[1, index - 1]
    rows, width = p.shape

    def around(v):
        return (
            pltpu.roll(v, rows - 1, 0),
            pltpu.roll(v, 1, 0),
            pltpu.roll(v, width - 1, 1),
            pltpu.roll(v, 1, 1),
        )

    pxp, pxm, pyp, pym = around(p)
    grad_z = 0.5 * (pzp - pzm)
    grad_x = 0.5 * (pxp - pxm)
    grad_y = 0.5 * (pyp - pym)
    turned_x = (grad_x + grad_y) * half_root
    turned_y = (grad_x - grad_y) * half_root
    comp_x = jnp.where(grain, turned_x, grad_x)
    comp_y = jnp.where(grain, turned_y, grad_y)
    sq_x = comp_x * comp_x
    sq_y = comp_y * comp_y
    sq_z = grad_z * grad_z
    total_sq = sq_x + sq_y + sq_z
    quartic = sq_x * sq_x + sq_y * sq_y + sq_z * sq_z
    floored = jnp.maximum(total_sq, grad_floor)
    aniso = 1.0 + aniso_strength * (4.0 * quartic / (floored * floored) - 3.0)
    aniso_sq = aniso * aniso
    laplace = pzp + pzm + pxp + pxm + pyp + pym - 6.0 * p
    left = 1.0 - p * p
    drive = p - p * p * p - coupling * (left * left) * (u + theta)
    rate = laplace + drive / aniso_sq
    clipped = clip(p)
    base = 2.0 - clipped
    flux = (base - clip(pzp)) * (uzp - u) + (base - clip(pzm)) * (uzm - u)
    for pn, un in zip((pxp, pxm, pyp, pym), around(u)):
        flux = flux + (base - clip(pn)) * (un - u)
    weight = 0.5 * (1.0 + partition - (1.0 - partition) * clipped)
    urate = (0.25 * flux + 0.5 * (1.0 + (1.0 - partition) * u) * rate) / weight
    return p + time_step * rate, u + time_step * urate


def kernel(
    lat_count, grow_count, phase_in, solute_in, grain_in, writer_in,
    phase_out, solute_out, check_out,
    to_left, to_right, from_left, from_right, ext, mid, fin, pieces, landed,
    left_send, right_send, left_recv, right_recv, z_send, z_recv, out_send, out_recv,
    piece_send, piece_recv, phase, solute, load_sem,
    grain_ref, writer, small_sem, blank, blank_sem,
):
    planes, rows, width = phase.shape
    quarter = planes // 4

    def loads(k):
        part = pl.ds(quarter * k, quarter)
        return (
            pltpu.make_async_copy(phase_in.at[part], phase.at[part], load_sem.at[0, k]),
            pltpu.make_async_copy(solute_in.at[part], solute.at[part], load_sem.at[1, k]),
        )

    for k in (3, 0, 1, 2):
        for copy in loads(k):
            copy.start()
    small = (
        pltpu.make_async_copy(grain_in, grain_ref, small_sem.at[0]),
        pltpu.make_async_copy(writer_in, writer, small_sem.at[1]),
    )
    for copy in small:
        copy.start()

    lat = lax.axis_index("lat")
    grow = lax.axis_index("grow")
    left = lax.rem(lat + lat_count - 1, lat_count)
    right = lax.rem(lat + 1, lat_count)
    top = grow == grow_count - 1
    bottom = grow == 0
    total = planes * grow_count
    pairs = planes // 2

    barrier = pltpu.get_barrier_semaphore()

    def greet(a, b):
        pl.semaphore_signal(barrier, inc=1, device_id=(a, b), device_id_type=MESH)

    @pl.when(bottom)
    def _():
        def one(k, carry):
            peer = lax.rem(lat + k, lat_count)
            for r in range(grow_count):
                if r == 0:
                    @pl.when(k > 0)
                    def _():
                        greet(peer, r)
                else:
                    greet(peer, r)
            return carry
        lax.fori_loop(0, lat_count, one, 0)

    @pl.when(grow > 0)
    def _():
        def one(k, carry):
            greet(lax.rem(lat + k, lat_count), 0)
            return carry
        lax.fori_loop(0, lat_count, one, 0)
        greet(left, grow)
        greet(right, grow)

        @pl.when(grow > 1)
        def _():
            greet(lat, grow - 1)

        @pl.when(grow < grow_count - 1)
        def _():
            greet(lat, grow + 1)

    def pack(z, carry):
        to_right[z, 0:2, :] = phase[z, rows - 2 : rows, :]
        to_right[z, 2:4, :] = solute[z, rows - 2 : rows, :]
        to_left[z, 0:2, :] = phase[z, 0:2, :]
        to_left[z, 2:4, :] = solute[z, 0:2, :]
        return carry

    for k in (3, 0, 1, 2):
        for copy in loads(k):
            copy.wait()
        lax.fori_loop(quarter * k, quarter * (k + 1), pack, 0)

    @pl.when(bottom)
    def _():
        pl.semaphore_wait(barrier, lat_count * grow_count - 1)

    @pl.when(grow > 0)
    def _():
        pl.semaphore_wait(barrier, lat_count + 2)

        @pl.when(grow > 1)
        def _():
            pl.semaphore_wait(barrier, 1)

        @pl.when(grow < grow_count - 1)
        def _():
            pl.semaphore_wait(barrier, 1)

    def sides(chunk):
        part = pl.ds(2 * chunk, 2)
        return (
            pltpu.make_async_remote_copy(
                src_ref=to_right.at[part], dst_ref=from_left.at[part],
                send_sem=right_send.at[chunk], recv_sem=left_recv.at[chunk],
                device_id=(right, grow), device_id_type=MESH),
            pltpu.make_async_remote_copy(
                src_ref=to_left.at[part], dst_ref=from_right.at[part],
                send_sem=left_send.at[chunk], recv_sem=right_recv.at[chunk],
                device_id=(left, grow), device_id_type=MESH),
        )

    def begin(k, carry):
        for copy in sides(lax.rem(k + pairs - 1, pairs)):
            copy.start()
        return carry

    lax.fori_loop(0, pairs, begin, 0)

    def own(z, carry):
        ext[0, z + 2, 2 : 2 + rows, :] = phase[z]
        ext[1, z + 2, 2 : 2 + rows, :] = solute[z]
        return carry

    lax.fori_loop(0, planes, own, 0)

    for copy in small:
        copy.wait()

    def blanks():
        return [
            pltpu.make_async_copy(blank.at[f], out.at[pl.ds(quarter * k, quarter)], blank_sem.at[f, k])
            for f, out in enumerate((phase_out, solute_out)) for k in range(4)
        ]

    @pl.when(top)
    def _():
        blank[0] = jnp.full(blank.shape[1:], -1.0, jnp.float32)
        blank[1] = jnp.full(blank.shape[1:], liquid_u, jnp.float32)
        for copy in blanks():
            copy.start()

    grain = jnp.broadcast_to(grain_ref[...].reshape(1, width), (rows + 4, width)) > 0

    def up_copy():
        return pltpu.make_async_remote_copy(
            src_ref=ext.at[:, pl.ds(planes, 2)], dst_ref=ext.at[:, pl.ds(0, 2)],
            send_sem=z_send.at[0], recv_sem=z_recv.at[0],
            device_id=(lat, jnp.minimum(grow + 1, grow_count - 1)), device_id_type=MESH)

    def down_copy():
        return pltpu.make_async_remote_copy(
            src_ref=ext.at[:, pl.ds(2, 2)], dst_ref=ext.at[:, pl.ds(planes + 2, 2)],
            send_sem=z_send.at[1], recv_sem=z_recv.at[1],
            device_id=(lat, jnp.maximum(grow - 1, 0)), device_id_type=MESH)

    def out_copies(pair):
        part = pl.ds(2 * pair, 2)
        return [
            pltpu.make_async_remote_copy(
                src_ref=fin.at[f, part], dst_ref=(phase_out, solute_out)[f].at[part],
                send_sem=out_send.at[f, pair], recv_sem=out_recv.at[f, pair],
                device_id=(lat, jnp.maximum(grow - 1, 0)), device_id_type=MESH)
            for f in range(2)
        ]

    def level(z):
        return ((grow * planes + z).astype(jnp.float32) + 0.5) / total - 0.5

    def first(j, carry):
        e = lax.rem(j + planes, planes + 2) + 1
        new_p, new_u = advance(ext, e, grain, level(e - 2))
        mid[0, e - 1] = new_p
        mid[1, e - 1] = new_u
        return carry

    def second(pair, carry):
        def plane(z, inner):
            new_p, new_u = advance(mid, z + 1, grain, level(z))
            fin[0, z] = new_p[2 : 2 + rows]
            fin[1, z] = new_u[2 : 2 + rows]
            return inner
        lax.fori_loop(2 * pair, 2 * pair + 2, plane, 0)

        @pl.when(grow > 0)
        def _():
            for copy in out_copies(pair):
                copy.start()
        return carry

    def fill(target, start, count, values):
        for f in range(2):
            target[f, start : start + count] = jnp.full(
                (count,) + target.shape[2:], values[f], jnp.float32)

    def turn(i, carry):
        chunk = lax.rem(i + pairs - 1, pairs)
        for copy in sides(chunk):
            copy.wait_recv()
        for k in range(2):
            z = 2 * chunk + k
            for f in range(2):
                ext[f, z + 2, 0:2, :] = from_left[z, 2 * f : 2 * f + 2, :]
                ext[f, z + 2, 2 + rows : 4 + rows, :] = from_right[z, 2 * f : 2 * f + 2, :]

        @pl.when((i == 0) & jnp.logical_not(top))
        def _():
            up_copy().start()

        @pl.when(i == 1)
        def _():
            @pl.when(grow > 0)
            def _():
                down_copy().start()

            @pl.when(bottom)
            def _():
                fill(ext, 0, 2, (1.0, solid_u))

            @pl.when(top)
            def _():
                fill(ext, planes + 2, 2, (-1.0, liquid_u))

            @pl.when(grow > 0)
            def _():
                up_copy().wait_recv()

            @pl.when(jnp.logical_not(top))
            def _():
                down_copy().wait_recv()

        low = jnp.where(i <= 1, 0, 2 * i)
        high = jnp.where(i == 0, 0, jnp.where(i == pairs - 1, planes + 2, 2 * i + 2))
        lax.fori_loop(low, high, first, 0)

        @pl.when(i == 1)
        def _():
            @pl.when(bottom)
            def _():
                fill(mid, 0, 1, (1.0, solid_u))

            @pl.when(top)
            def _():
                fill(mid, planes + 1, 1, (-1.0, liquid_u))

        low = jnp.maximum(i - 2, 0)
        high = jnp.where(i == pairs - 1, pairs, jnp.maximum(i - 1, 0))
        lax.fori_loop(low, high, second, 0)
        return carry

    lax.fori_loop(0, pairs, turn, 0)

    span = width // grow_count
    lanes = pieces.shape[2]

    @pl.when(bottom)
    def _():
        sums = []
        for f in range(2):
            for group in range(planes // 4):
                four = fin[f, 4 * group] + fin[f, 4 * group + 1]
                four = four + fin[f, 4 * group + 2] + fin[f, 4 * group + 3]
                sums.append(jnp.sum(four, axis=0, keepdims=True))
        sums = jnp.concatenate(sums, axis=0) * (1.0 / 64.0)
        cell = lax.broadcasted_iota(jnp.int32, (span, lanes), 0)
        lane = lax.broadcasted_iota(jnp.int32, (span, lanes), 1)
        pick = jnp.where((cell >= 4 * lane) & (cell < 4 * lane + 4), 1.0, 0.0).astype(jnp.bfloat16)
        high = sums.astype(jnp.bfloat16).astype(jnp.float32)
        rest = sums - high
        middle = rest.astype(jnp.bfloat16).astype(jnp.float32)
        low = rest - middle
        count = sums.shape[0]
        parts = jnp.concatenate([high, middle, low, jnp.zeros_like(low)], axis=0).astype(jnp.bfloat16)
        for r in range(grow_count):
            out = jnp.dot(parts[:, r * span : (r + 1) * span], pick, preferred_element_type=jnp.float32)
            pieces[r] = out[0:count] + out[count : 2 * count] + out[2 * count : 3 * count]
        landed[lat] = pieces[0]

        def send(k, carry):
            peer = lax.rem(lat + k, lat_count)
            for r in range(grow_count):
                def go(r=r):
                    pltpu.make_async_remote_copy(
                        src_ref=pieces.at[r], dst_ref=landed.at[lat],
                        send_sem=piece_send.at[r], recv_sem=piece_recv,
                        device_id=(peer, r), device_id_type=MESH).start()
                if r == 0:
                    pl.when(k > 0)(go)
                else:
                    go()
            return carry
        lax.fori_loop(0, lat_count, send, 0)

    def finish(k, carry):
        for copy in sides(k):
            copy.wait_send()

        @pl.when(grow > 0)
        def _():
            for copy in out_copies(k):
                copy.wait_send()

        @pl.when(jnp.logical_not(top))
        def _():
            for copy in out_copies(k):
                copy.wait_recv()
        return carry

    lax.fori_loop(0, pairs, finish, 0)

    @pl.when(top)
    def _():
        for copy in blanks():
            copy.wait()

    @pl.when(jnp.logical_not(top))
    def _():
        up_copy().wait_send()

    @pl.when(grow > 0)
    def _():
        down_copy().wait_send()

    others = landed.at[pl.ds(0, lat_count - 1)]

    @pl.when(bottom)
    def _():
        pltpu.make_async_copy(others, others, piece_recv).wait()

    @pl.when(grow > 0)
    def _():
        pltpu.make_async_copy(landed, landed, piece_recv).wait()

    def find(k, found):
        return jnp.where(writer[grow, k] == lat, k, found)

    mine = landed[lax.fori_loop(0, lat_count, find, 0)]
    for f in range(2):
        for group in range(planes // 4):
            at = f * (planes // 4) + group
            check_out[0, 0, f, group] = mine[at : at + 1, 0 : check_out.shape[5]]

    @pl.when(bottom)
    def _():
        pltpu.make_async_copy(others, others, piece_send.at[0]).wait()
        for r in range(1, grow_count):
            pltpu.make_async_copy(landed, landed, piece_send.at[r]).wait()


def store(phase, solute, check, phase_out, solute_out, check_out, sems, last):
    count = sems.shape[1]
    size = phase.shape[0] // count
    copies = [pltpu.make_async_copy(check, check_out, last)]
    for k in range(count):
        part = pl.ds(k * size, size)
        copies.append(pltpu.make_async_copy(phase.at[part], phase_out.at[part], sems.at[0, k]))
        copies.append(pltpu.make_async_copy(solute.at[part], solute_out.at[part], sems.at[1, k]))
    for copy in copies:
        copy.start()
    for copy in copies:
        copy.wait()


def shards(phase, solute, seed_grain, writer):
    planes, rows, width = phase.shape
    lat_count = lax.axis_size("lat")
    grow_count = lax.axis_size("grow")
    piece = width // 4 // grow_count
    lanes = -(-piece // 128) * 128
    wide = rows + 4
    pairs = planes // 2
    f32 = jnp.float32
    dma = pltpu.SemaphoreType.DMA
    vmem = pl.BlockSpec(memory_space=pltpu.VMEM)
    anywhere = pl.BlockSpec(memory_space=pltpu.HBM)
    results = pl.pallas_call(
        functools.partial(kernel, lat_count, grow_count),
        out_shape=(
            pltpu.VMEM(phase.shape, f32),
            pltpu.VMEM(phase.shape, f32),
            pltpu.VMEM((1, 1, 2, planes // 4, rows // 4, piece), f32),
        ),
        in_specs=[anywhere] * 4,
        out_specs=(vmem, vmem, vmem),
        scratch_shapes=[
            pltpu.VMEM((planes, 4, width), f32),
            pltpu.VMEM((planes, 4, width), f32),
            pltpu.VMEM((planes, 4, width), f32),
            pltpu.VMEM((planes, 4, width), f32),
            pltpu.VMEM((2, planes + 4, wide, width), f32),
            pltpu.VMEM((2, planes + 2, wide, width), f32),
            pltpu.VMEM((2, planes, rows, width), f32),
            pltpu.VMEM((grow_count, planes // 2, lanes), f32),
            pltpu.VMEM((lat_count, planes // 2, lanes), f32),
            dma((pairs,)), dma((pairs,)), dma((pairs,)), dma((pairs,)),
            dma((2,)), dma((2,)), dma((2, pairs)), dma((2, pairs)),
            dma((grow_count,)), dma,
            pltpu.VMEM(phase.shape, f32),
            pltpu.VMEM(phase.shape, f32),
            dma((2, 4)),
            pltpu.VMEM(seed_grain.shape, jnp.int32),
            pltpu.SMEM(writer.shape, jnp.int32),
            dma((2,)),
            pltpu.VMEM((2, planes // 4, rows, width), f32),
            dma((2, 4)),
        ],
        compiler_params=pltpu.CompilerParams(
            collective_id=0, has_side_effects=True, vmem_limit_bytes=vmem_bytes),
    )(phase, solute, seed_grain, writer)
    return tuple(pl.pallas_call(
        store,
        out_shape=tuple(jax.ShapeDtypeStruct(r.shape, f32) for r in results),
        in_specs=[vmem] * 3,
        out_specs=(anywhere,) * 3,
        scratch_shapes=[dma((2, 8)), dma],
        compiler_params=pltpu.CompilerParams(vmem_limit_bytes=8 * 1024 * 1024),
    )(*results))


def solution(mesh):
    placed = (P("grow", "lat", None), P("grow", "lat", None), P(), P())
    return jax.shard_map(
        shards,
        mesh=mesh,
        in_specs=placed,
        out_specs=(
            P("grow", "lat", None),
            P("grow", "lat", None),
            P("grow", "lat", None, None, None, None),
        ),
        check_vma=False,
    )
```

```python
import functools

import jax
import jax.numpy as jnp
from jax import lax
from jax.experimental import pallas as pl
from jax.experimental.pallas import tpu as pltpu
from jax.sharding import PartitionSpec as P

time_step = 0.15
aniso_strength = 0.15
coupling = 3.0
partition = 0.15
grad_floor = 0.25
solid_u = -0.5
liquid_u = 0.0
half_root = 0.7071067811865476
MESH = pl.DeviceIdType.MESH
vmem_bytes = 62 * 1024 * 1024


def clip(v):
    return jnp.minimum(jnp.maximum(v, -1.0), 1.0)


def advance(fields, index, grain, theta):
    p = fields[0, index]
    u = fields[1, index]
    pzp = fields[0, index + 1]
    pzm = fields[0, index - 1]
    uzp = fields[1, index + 1]
    uzm = fields[1, index - 1]
    rows, width = p.shape

    def around(v):
        return (
            pltpu.roll(v, rows - 1, 0),
            pltpu.roll(v, 1, 0),
            pltpu.roll(v, width - 1, 1),
            pltpu.roll(v, 1, 1),
        )

    pxp, pxm, pyp, pym = around(p)
    grad_z = 0.5 * (pzp - pzm)
    grad_x = 0.5 * (pxp - pxm)
    grad_y = 0.5 * (pyp - pym)
    turned_x = (grad_x + grad_y) * half_root
    turned_y = (grad_x - grad_y) * half_root
    comp_x = jnp.where(grain, turned_x, grad_x)
    comp_y = jnp.where(grain, turned_y, grad_y)
    sq_x = comp_x * comp_x
    sq_y = comp_y * comp_y
    sq_z = grad_z * grad_z
    total_sq = sq_x + sq_y + sq_z
    quartic = sq_x * sq_x + sq_y * sq_y + sq_z * sq_z
    floored = jnp.maximum(total_sq, grad_floor)
    aniso = 1.0 + aniso_strength * (4.0 * quartic / (floored * floored) - 3.0)
    aniso_sq = aniso * aniso
    laplace = pzp + pzm + pxp + pxm + pyp + pym - 6.0 * p
    left = 1.0 - p * p
    drive = p - p * p * p - coupling * (left * left) * (u + theta)
    rate = laplace + drive / aniso_sq
    clipped = clip(p)
    base = 2.0 - clipped
    flux = (base - clip(pzp)) * (uzp - u) + (base - clip(pzm)) * (uzm - u)
    for pn, un in zip((pxp, pxm, pyp, pym), around(u)):
        flux = flux + (base - clip(pn)) * (un - u)
    weight = 0.5 * (1.0 + partition - (1.0 - partition) * clipped)
    urate = (0.25 * flux + 0.5 * (1.0 + (1.0 - partition) * u) * rate) / weight
    return p + time_step * rate, u + time_step * urate


def kernel(
    lat_count, grow_count, phase_in, solute_in, grain_in, writer_in,
    phase_out, solute_out, check_out,
    to_left, to_right, from_left, from_right, ext, mid, fin, pieces, landed,
    left_send, right_send, left_recv, right_recv, z_send, z_recv, out_send, out_recv,
    piece_send, piece_recv, phase, solute, load_sem,
    grain_ref, writer, small_sem, blank, blank_sem, pick,
):
    planes, rows, width = phase.shape
    quarter = planes // 4

    def loads(k):
        part = pl.ds(quarter * k, quarter)
        return (
            pltpu.make_async_copy(phase_in.at[part], phase.at[part], load_sem.at[0, k]),
            pltpu.make_async_copy(solute_in.at[part], solute.at[part], load_sem.at[1, k]),
        )

    for k in (3, 0, 1, 2):
        for copy in loads(k):
            copy.start()
    small = (
        pltpu.make_async_copy(grain_in, grain_ref, small_sem.at[0]),
        pltpu.make_async_copy(writer_in, writer, small_sem.at[1]),
    )
    for copy in small:
        copy.start()

    lat = lax.axis_index("lat")
    grow = lax.axis_index("grow")
    left = lax.rem(lat + lat_count - 1, lat_count)
    right = lax.rem(lat + 1, lat_count)
    top = grow == grow_count - 1
    bottom = grow == 0
    total = planes * grow_count
    pairs = planes // 2

    barrier = pltpu.get_barrier_semaphore()

    def greet(a, b):
        pl.semaphore_signal(barrier, inc=1, device_id=(a, b), device_id_type=MESH)

    @pl.when(bottom)
    def _():
        def one(k, carry):
            peer = lax.rem(lat + k, lat_count)
            for r in range(grow_count):
                if r == 0:
                    @pl.when(k > 0)
                    def _():
                        greet(peer, r)
                else:
                    greet(peer, r)
            return carry
        lax.fori_loop(0, lat_count, one, 0)

    @pl.when(grow > 0)
    def _():
        def one(k, carry):
            greet(lax.rem(lat + k, lat_count), 0)
            return carry
        lax.fori_loop(0, lat_count, one, 0)
        greet(left, grow)
        greet(right, grow)

        @pl.when(grow > 1)
        def _():
            greet(lat, grow - 1)

        @pl.when(grow < grow_count - 1)
        def _():
            greet(lat, grow + 1)

    def pack(z, carry):
        to_right[z, 0:2, :] = phase[z, rows - 2 : rows, :]
        to_right[z, 2:4, :] = solute[z, rows - 2 : rows, :]
        to_left[z, 0:2, :] = phase[z, 0:2, :]
        to_left[z, 2:4, :] = solute[z, 0:2, :]
        return carry

    for k in (3, 0, 1, 2):
        for copy in loads(k):
            copy.wait()
        lax.fori_loop(quarter * k, quarter * (k + 1), pack, 0)

    @pl.when(bottom)
    def _():
        pl.semaphore_wait(barrier, lat_count * grow_count - 1)

    @pl.when(grow > 0)
    def _():
        pl.semaphore_wait(barrier, lat_count + 2)

        @pl.when(grow > 1)
        def _():
            pl.semaphore_wait(barrier, 1)

        @pl.when(grow < grow_count - 1)
        def _():
            pl.semaphore_wait(barrier, 1)

    def sides(chunk):
        part = pl.ds(2 * chunk, 2)
        return (
            pltpu.make_async_remote_copy(
                src_ref=to_right.at[part], dst_ref=from_left.at[part],
                send_sem=right_send.at[chunk], recv_sem=left_recv.at[chunk],
                device_id=(right, grow), device_id_type=MESH),
            pltpu.make_async_remote_copy(
                src_ref=to_left.at[part], dst_ref=from_right.at[part],
                send_sem=left_send.at[chunk], recv_sem=right_recv.at[chunk],
                device_id=(left, grow), device_id_type=MESH),
        )

    def begin(k, carry):
        for copy in sides(lax.rem(k + pairs - 1, pairs)):
            copy.start()
        return carry

    lax.fori_loop(0, pairs, begin, 0)

    def own(z, carry):
        ext[0, z + 2, 2 : 2 + rows, :] = phase[z]
        ext[1, z + 2, 2 : 2 + rows, :] = solute[z]
        return carry

    lax.fori_loop(0, planes, own, 0)

    for copy in small:
        copy.wait()

    def blanks():
        return [
            pltpu.make_async_copy(blank.at[f], out.at[pl.ds(quarter * k, quarter)], blank_sem.at[f, k])
            for f, out in enumerate((phase_out, solute_out)) for k in range(4)
        ]

    @pl.when(top)
    def _():
        blank[0] = jnp.full(blank.shape[1:], -1.0, jnp.float32)
        blank[1] = jnp.full(blank.shape[1:], liquid_u, jnp.float32)
        for copy in blanks():
            copy.start()

    grain = jnp.broadcast_to(grain_ref[...].reshape(1, width), (rows + 4, width)) > 0

    def up_copy():
        return pltpu.make_async_remote_copy(
            src_ref=ext.at[:, pl.ds(planes, 2)], dst_ref=ext.at[:, pl.ds(0, 2)],
            send_sem=z_send.at[0], recv_sem=z_recv.at[0],
            device_id=(lat, jnp.minimum(grow + 1, grow_count - 1)), device_id_type=MESH)

    def down_copy():
        return pltpu.make_async_remote_copy(
            src_ref=ext.at[:, pl.ds(2, 2)], dst_ref=ext.at[:, pl.ds(planes + 2, 2)],
            send_sem=z_send.at[1], recv_sem=z_recv.at[1],
            device_id=(lat, jnp.maximum(grow - 1, 0)), device_id_type=MESH)

    def out_copies(pair):
        part = pl.ds(2 * pair, 2)
        return [
            pltpu.make_async_remote_copy(
                src_ref=fin.at[f, part], dst_ref=(phase_out, solute_out)[f].at[part],
                send_sem=out_send.at[f, pair], recv_sem=out_recv.at[f, pair],
                device_id=(lat, jnp.maximum(grow - 1, 0)), device_id_type=MESH)
            for f in range(2)
        ]

    def level(z):
        return ((grow * planes + z).astype(jnp.float32) + 0.5) / total - 0.5

    def first(j, carry):
        e = lax.rem(j + planes, planes + 2) + 1
        new_p, new_u = advance(ext, e, grain, level(e - 2))
        mid[0, e - 1] = new_p
        mid[1, e - 1] = new_u
        return carry

    def second(pair, carry):
        def plane(z, inner):
            new_p, new_u = advance(mid, z + 1, grain, level(z))
            fin[0, z] = new_p[2 : 2 + rows]
            fin[1, z] = new_u[2 : 2 + rows]
            return inner
        lax.fori_loop(2 * pair, 2 * pair + 2, plane, 0)

        @pl.when(grow > 0)
        def _():
            for copy in out_copies(pair):
                copy.start()
        return carry

    span = width // grow_count
    lanes = pieces.shape[3]
    groups = planes // 8
    cell = lax.broadcasted_iota(jnp.int32, (span, lanes), 0)
    lane = lax.broadcasted_iota(jnp.int32, (span, lanes), 1)
    pick[...] = jnp.where((cell >= 4 * lane) & (cell < 4 * lane + 4), 1.0, 0.0).astype(jnp.bfloat16)

    def coarsen(half):
        sums = []
        for f in range(2):
            for group in range(groups):
                z = (half * groups + group) * 4
                four = fin[f, z] + fin[f, z + 1] + fin[f, z + 2] + fin[f, z + 3]
                sums.append(jnp.sum(four, axis=0, keepdims=True))
        sums = jnp.concatenate(sums, axis=0) * (1.0 / 64.0)
        high = sums.astype(jnp.bfloat16).astype(jnp.float32)
        rest = sums - high
        middle = rest.astype(jnp.bfloat16).astype(jnp.float32)
        low = rest - middle
        count = sums.shape[0]
        parts = jnp.concatenate([high, middle, low, jnp.zeros_like(low)], axis=0).astype(jnp.bfloat16)
        for r in range(grow_count):
            out = jnp.dot(parts[:, r * span : (r + 1) * span], pick[...], preferred_element_type=jnp.float32)
            out = out[0:count] + out[count : 2 * count] + out[2 * count : 3 * count]
            pieces[half, r] = out
            if r == 0:
                landed[half, lat] = out

        def send(k, carry):
            peer = lax.rem(lat + k, lat_count)
            for r in range(grow_count):
                def go(r=r):
                    pltpu.make_async_remote_copy(
                        src_ref=pieces.at[half, r], dst_ref=landed.at[half, lat],
                        send_sem=piece_send.at[half, r], recv_sem=piece_recv.at[half],
                        device_id=(peer, r), device_id_type=MESH).start()
                if r == 0:
                    pl.when(k > 0)(go)
                else:
                    go()
            return carry
        lax.fori_loop(0, lat_count, send, 0)

    def fill(target, start, count, values):
        for f in range(2):
            target[f, start : start + count] = jnp.full(
                (count,) + target.shape[2:], values[f], jnp.float32)

    def turn(i, carry):
        chunk = lax.rem(i + pairs - 1, pairs)
        for copy in sides(chunk):
            copy.wait_recv()
        for k in range(2):
            z = 2 * chunk + k
            for f in range(2):
                ext[f, z + 2, 0:2, :] = from_left[z, 2 * f : 2 * f + 2, :]
                ext[f, z + 2, 2 + rows : 4 + rows, :] = from_right[z, 2 * f : 2 * f + 2, :]

        @pl.when((i == 0) & jnp.logical_not(top))
        def _():
            up_copy().start()

        @pl.when(i == 1)
        def _():
            @pl.when(grow > 0)
            def _():
                down_copy().start()

            @pl.when(bottom)
            def _():
                fill(ext, 0, 2, (1.0, solid_u))

            @pl.when(top)
            def _():
                fill(ext, planes + 2, 2, (-1.0, liquid_u))

            @pl.when(grow > 0)
            def _():
                up_copy().wait_recv()

            @pl.when(jnp.logical_not(top))
            def _():
                down_copy().wait_recv()

        low = jnp.where(i <= 1, 0, 2 * i)
        high = jnp.where(i == 0, 0, jnp.where(i == pairs - 1, planes + 2, 2 * i + 2))
        lax.fori_loop(low, high, first, 0)

        @pl.when(i == 1)
        def _():
            @pl.when(bottom)
            def _():
                fill(mid, 0, 1, (1.0, solid_u))

            @pl.when(top)
            def _():
                fill(mid, planes + 1, 1, (-1.0, liquid_u))

        low = jnp.maximum(i - 2, 0)
        high = jnp.where(i == pairs - 1, pairs, jnp.maximum(i - 1, 0))
        lax.fori_loop(low, high, second, 0)

        @pl.when(bottom & ((i == planes // 4 + 1) | (i == pairs - 1)))
        def _():
            coarsen(jnp.where(i == pairs - 1, 1, 0))
        return carry

    lax.fori_loop(0, pairs, turn, 0)

    def finish(k, carry):
        for copy in sides(k):
            copy.wait_send()

        @pl.when(grow > 0)
        def _():
            for copy in out_copies(k):
                copy.wait_send()

        @pl.when(jnp.logical_not(top))
        def _():
            for copy in out_copies(k):
                copy.wait_recv()
        return carry

    lax.fori_loop(0, pairs, finish, 0)

    @pl.when(top)
    def _():
        for copy in blanks():
            copy.wait()

    @pl.when(jnp.logical_not(top))
    def _():
        up_copy().wait_send()

    @pl.when(grow > 0)
    def _():
        down_copy().wait_send()

    def others(half):
        return landed.at[half, pl.ds(0, lat_count - 1)]

    @pl.when(bottom)
    def _():
        for half in range(2):
            pltpu.make_async_copy(others(half), others(half), piece_recv.at[half]).wait()

    @pl.when(grow > 0)
    def _():
        for half in range(2):
            pltpu.make_async_copy(landed.at[half], landed.at[half], piece_recv.at[half]).wait()

    def find(k, found):
        return jnp.where(writer[grow, k] == lat, k, found)

    origin = lax.fori_loop(0, lat_count, find, 0)
    for half in range(2):
        mine = landed[half, origin]
        for f in range(2):
            for group in range(groups):
                at = f * groups + group
                check_out[0, 0, f, half * groups + group] = mine[at : at + 1, 0 : check_out.shape[5]]

    @pl.when(bottom)
    def _():
        for half in range(2):
            pltpu.make_async_copy(others(half), others(half), piece_send.at[half, 0]).wait()
            for r in range(1, grow_count):
                pltpu.make_async_copy(landed.at[half], landed.at[half], piece_send.at[half, r]).wait()


def store(phase, solute, check, phase_out, solute_out, check_out, sems, last):
    count = sems.shape[1]
    size = phase.shape[0] // count
    copies = [pltpu.make_async_copy(check, check_out, last)]
    for k in range(count):
        part = pl.ds(k * size, size)
        copies.append(pltpu.make_async_copy(phase.at[part], phase_out.at[part], sems.at[0, k]))
        copies.append(pltpu.make_async_copy(solute.at[part], solute_out.at[part], sems.at[1, k]))
    for copy in copies:
        copy.start()
    for copy in copies:
        copy.wait()


def shards(phase, solute, seed_grain, writer):
    planes, rows, width = phase.shape
    lat_count = lax.axis_size("lat")
    grow_count = lax.axis_size("grow")
    piece = width // 4 // grow_count
    lanes = -(-piece // 128) * 128
    wide = rows + 4
    pairs = planes // 2
    f32 = jnp.float32
    dma = pltpu.SemaphoreType.DMA
    vmem = pl.BlockSpec(memory_space=pltpu.VMEM)
    anywhere = pl.BlockSpec(memory_space=pltpu.HBM)
    results = pl.pallas_call(
        functools.partial(kernel, lat_count, grow_count),
        out_shape=(
            pltpu.VMEM(phase.shape, f32),
            pltpu.VMEM(phase.shape, f32),
            pltpu.VMEM((1, 1, 2, planes // 4, rows // 4, piece), f32),
        ),
        in_specs=[anywhere] * 4,
        out_specs=(vmem, vmem, vmem),
        scratch_shapes=[
            pltpu.VMEM((planes, 4, width), f32),
            pltpu.VMEM((planes, 4, width), f32),
            pltpu.VMEM((planes, 4, width), f32),
            pltpu.VMEM((planes, 4, width), f32),
            pltpu.VMEM((2, planes + 4, wide, width), f32),
            pltpu.VMEM((2, planes + 2, wide, width), f32),
            pltpu.VMEM((2, planes, rows, width), f32),
            pltpu.VMEM((2, grow_count, planes // 4, lanes), f32),
            pltpu.VMEM((2, lat_count, planes // 4, lanes), f32),
            dma((pairs,)), dma((pairs,)), dma((pairs,)), dma((pairs,)),
            dma((2,)), dma((2,)), dma((2, pairs)), dma((2, pairs)),
            dma((2, grow_count)), dma((2,)),
            pltpu.VMEM(phase.shape, f32),
            pltpu.VMEM(phase.shape, f32),
            dma((2, 4)),
            pltpu.VMEM(seed_grain.shape, jnp.int32),
            pltpu.SMEM(writer.shape, jnp.int32),
            dma((2,)),
            pltpu.VMEM((2, planes // 4, rows, width), f32),
            dma((2, 4)),
            pltpu.VMEM((width // grow_count, lanes), jnp.bfloat16),
        ],
        compiler_params=pltpu.CompilerParams(
            collective_id=0, has_side_effects=True, vmem_limit_bytes=vmem_bytes),
    )(phase, solute, seed_grain, writer)
    return tuple(pl.pallas_call(
        store,
        out_shape=tuple(jax.ShapeDtypeStruct(r.shape, f32) for r in results),
        in_specs=[vmem] * 3,
        out_specs=(anywhere,) * 3,
        scratch_shapes=[dma((2, 8)), dma],
        compiler_params=pltpu.CompilerParams(vmem_limit_bytes=8 * 1024 * 1024),
    )(*results))


def solution(mesh):
    placed = (P("grow", "lat", None), P("grow", "lat", None), P(), P())
    return jax.shard_map(
        shards,
        mesh=mesh,
        in_specs=placed,
        out_specs=(
            P("grow", "lat", None),
            P("grow", "lat", None),
            P("grow", "lat", None, None, None, None),
        ),
        check_vma=False,
    )
```

```python
import functools

import jax
import jax.numpy as jnp
from jax import lax
from jax.experimental import pallas as pl
from jax.experimental.pallas import tpu as pltpu
from jax.sharding import PartitionSpec as P

time_step = 0.15
aniso_strength = 0.15
coupling = 3.0
partition = 0.15
grad_floor = 0.25
solid_u = -0.5
liquid_u = 0.0
half_root = 0.7071067811865476
MESH = pl.DeviceIdType.MESH
vmem_bytes = 62 * 1024 * 1024


def clip(v):
    return jnp.minimum(jnp.maximum(v, -1.0), 1.0)


def advance(fields, index, grain, theta):
    p = fields[0, index]
    u = fields[1, index]
    pzp = fields[0, index + 1]
    pzm = fields[0, index - 1]
    uzp = fields[1, index + 1]
    uzm = fields[1, index - 1]
    rows, width = p.shape

    def around(v):
        return (
            pltpu.roll(v, rows - 1, 0),
            pltpu.roll(v, 1, 0),
            pltpu.roll(v, width - 1, 1),
            pltpu.roll(v, 1, 1),
        )

    pxp, pxm, pyp, pym = around(p)
    grad_z = 0.5 * (pzp - pzm)
    grad_x = 0.5 * (pxp - pxm)
    grad_y = 0.5 * (pyp - pym)
    turned_x = (grad_x + grad_y) * half_root
    turned_y = (grad_x - grad_y) * half_root
    comp_x = jnp.where(grain, turned_x, grad_x)
    comp_y = jnp.where(grain, turned_y, grad_y)
    sq_x = comp_x * comp_x
    sq_y = comp_y * comp_y
    sq_z = grad_z * grad_z
    total_sq = sq_x + sq_y + sq_z
    quartic = sq_x * sq_x + sq_y * sq_y + sq_z * sq_z
    floored = jnp.maximum(total_sq, grad_floor)
    aniso = 1.0 + aniso_strength * (4.0 * quartic / (floored * floored) - 3.0)
    aniso_sq = aniso * aniso
    laplace = pzp + pzm + pxp + pxm + pyp + pym - 6.0 * p
    left = 1.0 - p * p
    drive = p - p * p * p - coupling * (left * left) * (u + theta)
    rate = laplace + drive / aniso_sq
    clipped = clip(p)
    base = 2.0 - clipped
    flux = (base - clip(pzp)) * (uzp - u) + (base - clip(pzm)) * (uzm - u)
    for pn, un in zip((pxp, pxm, pyp, pym), around(u)):
        flux = flux + (base - clip(pn)) * (un - u)
    weight = 0.5 * (1.0 + partition - (1.0 - partition) * clipped)
    urate = (0.25 * flux + 0.5 * (1.0 + (1.0 - partition) * u) * rate) / weight
    return p + time_step * rate, u + time_step * urate


def kernel(
    lat_count, grow_count, phase_in, solute_in, grain_in, writer_in,
    phase_out, solute_out, check_out,
    to_left, to_right, from_left, from_right, ext, mid, fin, pieces, landed,
    left_send, right_send, left_recv, right_recv, z_send, z_recv, out_send, out_recv,
    piece_send, piece_recv, phase, solute, load_sem,
    grain_ref, writer, small_sem, blank, blank_sem, pick,
):
    planes, rows, width = phase.shape
    quarter = planes // 4

    def loads(k):
        part = pl.ds(quarter * k, quarter)
        return (
            pltpu.make_async_copy(phase_in.at[part], phase.at[part], load_sem.at[0, k]),
            pltpu.make_async_copy(solute_in.at[part], solute.at[part], load_sem.at[1, k]),
        )

    for k in (3, 0, 1, 2):
        for copy in loads(k):
            copy.start()
    small = (
        pltpu.make_async_copy(grain_in, grain_ref, small_sem.at[0]),
        pltpu.make_async_copy(writer_in, writer, small_sem.at[1]),
    )
    for copy in small:
        copy.start()

    lat = lax.axis_index("lat")
    grow = lax.axis_index("grow")
    left = lax.rem(lat + lat_count - 1, lat_count)
    right = lax.rem(lat + 1, lat_count)
    top = grow == grow_count - 1
    bottom = grow == 0
    total = planes * grow_count
    pairs = planes // 2

    barrier = pltpu.get_barrier_semaphore()

    def greet(a, b):
        pl.semaphore_signal(barrier, inc=1, device_id=(a, b), device_id_type=MESH)

    @pl.when(bottom)
    def _():
        def one(k, carry):
            peer = lax.rem(lat + k, lat_count)
            for r in range(grow_count):
                if r == 0:
                    @pl.when(k > 0)
                    def _():
                        greet(peer, r)
                else:
                    greet(peer, r)
            return carry
        lax.fori_loop(0, lat_count, one, 0)

    @pl.when(grow > 0)
    def _():
        def one(k, carry):
            greet(lax.rem(lat + k, lat_count), 0)
            return carry
        lax.fori_loop(0, lat_count, one, 0)
        greet(left, grow)
        greet(right, grow)

        @pl.when(grow > 1)
        def _():
            greet(lat, grow - 1)

        @pl.when(grow < grow_count - 1)
        def _():
            greet(lat, grow + 1)

    def pack(z, carry):
        to_right[z, 0:2, :] = phase[z, rows - 2 : rows, :]
        to_right[z, 2:4, :] = solute[z, rows - 2 : rows, :]
        to_left[z, 0:2, :] = phase[z, 0:2, :]
        to_left[z, 2:4, :] = solute[z, 0:2, :]
        return carry

    for k in (3, 0, 1, 2):
        for copy in loads(k):
            copy.wait()
        lax.fori_loop(quarter * k, quarter * (k + 1), pack, 0)

    @pl.when(bottom)
    def _():
        pl.semaphore_wait(barrier, lat_count * grow_count - 1)

    @pl.when(grow > 0)
    def _():
        pl.semaphore_wait(barrier, lat_count + 2)

        @pl.when(grow > 1)
        def _():
            pl.semaphore_wait(barrier, 1)

        @pl.when(grow < grow_count - 1)
        def _():
            pl.semaphore_wait(barrier, 1)

    def sides(chunk):
        part = pl.ds(2 * chunk, 2)
        return (
            pltpu.make_async_remote_copy(
                src_ref=to_right.at[part], dst_ref=from_left.at[part],
                send_sem=right_send.at[chunk], recv_sem=left_recv.at[chunk],
                device_id=(right, grow), device_id_type=MESH),
            pltpu.make_async_remote_copy(
                src_ref=to_left.at[part], dst_ref=from_right.at[part],
                send_sem=left_send.at[chunk], recv_sem=right_recv.at[chunk],
                device_id=(left, grow), device_id_type=MESH),
        )

    def begin(k, carry):
        for copy in sides(lax.rem(k + pairs - 1, pairs)):
            copy.start()
        return carry

    lax.fori_loop(0, pairs, begin, 0)

    def own(z, carry):
        ext[0, z + 2, 2 : 2 + rows, :] = phase[z]
        ext[1, z + 2, 2 : 2 + rows, :] = solute[z]
        return carry

    lax.fori_loop(0, planes, own, 0)

    for copy in small:
        copy.wait()

    def blanks():
        return [
            pltpu.make_async_copy(blank.at[f], out.at[pl.ds(quarter * k, quarter)], blank_sem.at[f, k])
            for f, out in enumerate((phase_out, solute_out)) for k in range(4)
        ]

    @pl.when(top)
    def _():
        blank[0] = jnp.full(blank.shape[1:], -1.0, jnp.float32)
        blank[1] = jnp.full(blank.shape[1:], liquid_u, jnp.float32)
        for copy in blanks():
            copy.start()

    grain = jnp.broadcast_to(grain_ref[...].reshape(1, width), (rows + 4, width)) > 0

    def up_copy():
        return pltpu.make_async_remote_copy(
            src_ref=ext.at[:, pl.ds(planes, 2)], dst_ref=ext.at[:, pl.ds(0, 2)],
            send_sem=z_send.at[0], recv_sem=z_recv.at[0],
            device_id=(lat, jnp.minimum(grow + 1, grow_count - 1)), device_id_type=MESH)

    def down_copy():
        return pltpu.make_async_remote_copy(
            src_ref=ext.at[:, pl.ds(2, 2)], dst_ref=ext.at[:, pl.ds(planes + 2, 2)],
            send_sem=z_send.at[1], recv_sem=z_recv.at[1],
            device_id=(lat, jnp.maximum(grow - 1, 0)), device_id_type=MESH)

    def out_copies(pair):
        part = pl.ds(2 * pair, 2)
        return [
            pltpu.make_async_remote_copy(
                src_ref=fin.at[f, part], dst_ref=(phase_out, solute_out)[f].at[part],
                send_sem=out_send.at[f, pair], recv_sem=out_recv.at[f, pair],
                device_id=(lat, jnp.maximum(grow - 1, 0)), device_id_type=MESH)
            for f in range(2)
        ]

    def level(z):
        return ((grow * planes + z).astype(jnp.float32) + 0.5) / total - 0.5

    def first(j, carry):
        e = lax.rem(j + planes, planes + 2) + 1
        new_p, new_u = advance(ext, e, grain, level(e - 2))
        mid[0, e - 1] = new_p
        mid[1, e - 1] = new_u
        return carry

    def second(pair, carry):
        def plane(z, inner):
            new_p, new_u = advance(mid, z + 1, grain, level(z))
            fin[0, z] = new_p[2 : 2 + rows]
            fin[1, z] = new_u[2 : 2 + rows]
            return inner
        lax.fori_loop(2 * pair, 2 * pair + 2, plane, 0)

        @pl.when(grow > 0)
        def _():
            for copy in out_copies(pair):
                copy.start()
        return carry

    span = width // grow_count
    lanes = pieces.shape[3]
    groups = planes // 8
    cell = lax.broadcasted_iota(jnp.int32, (span, lanes), 0)
    lane = lax.broadcasted_iota(jnp.int32, (span, lanes), 1)
    pick[...] = jnp.where((cell >= 4 * lane) & (cell < 4 * lane + 4), 1.0, 0.0).astype(jnp.bfloat16)

    def coarsen(half):
        sums = []
        for f in range(2):
            for group in range(groups):
                z = (half * groups + group) * 4
                four = fin[f, z] + fin[f, z + 1] + fin[f, z + 2] + fin[f, z + 3]
                sums.append(jnp.sum(four, axis=0, keepdims=True))
        sums = jnp.concatenate(sums, axis=0) * (1.0 / 64.0)
        high = sums.astype(jnp.bfloat16).astype(jnp.float32)
        rest = sums - high
        middle = rest.astype(jnp.bfloat16).astype(jnp.float32)
        low = rest - middle
        count = sums.shape[0]
        parts = jnp.concatenate([high, middle, low, jnp.zeros_like(low)], axis=0).astype(jnp.bfloat16)
        for r in range(grow_count):
            out = jnp.dot(parts[:, r * span : (r + 1) * span], pick[...], preferred_element_type=jnp.float32)
            out = out[0:count] + out[count : 2 * count] + out[2 * count : 3 * count]
            pieces[half, r] = out
            if r == 0:
                landed[half, lat] = out

        def send(k, carry):
            peer = lax.rem(lat + k, lat_count)
            for r in range(grow_count):
                def go(r=r):
                    pltpu.make_async_remote_copy(
                        src_ref=pieces.at[half, r], dst_ref=landed.at[half, lat],
                        send_sem=piece_send.at[half, r], recv_sem=piece_recv.at[half],
                        device_id=(peer, r), device_id_type=MESH).start()
                if r == 0:
                    pl.when(k > 0)(go)
                else:
                    go()
            return carry
        several = 4 if lat_count % 4 == 0 else 1

        def send_several(q, carry):
            for j in range(several):
                send(q * several + j, carry)
            return carry
        lax.fori_loop(0, lat_count // several, send_several, 0)

    def fill(target, start, count, values):
        for f in range(2):
            target[f, start : start + count] = jnp.full(
                (count,) + target.shape[2:], values[f], jnp.float32)

    def turn(i, carry):
        chunk = lax.rem(i + pairs - 1, pairs)
        for copy in sides(chunk):
            copy.wait_recv()
        for k in range(2):
            z = 2 * chunk + k
            for f in range(2):
                ext[f, z + 2, 0:2, :] = from_left[z, 2 * f : 2 * f + 2, :]
                ext[f, z + 2, 2 + rows : 4 + rows, :] = from_right[z, 2 * f : 2 * f + 2, :]

        @pl.when((i == 0) & jnp.logical_not(top))
        def _():
            up_copy().start()

        @pl.when(i == 1)
        def _():
            @pl.when(grow > 0)
            def _():
                down_copy().start()

            @pl.when(bottom)
            def _():
                fill(ext, 0, 2, (1.0, solid_u))

            @pl.when(top)
            def _():
                fill(ext, planes + 2, 2, (-1.0, liquid_u))

            @pl.when(grow > 0)
            def _():
                up_copy().wait_recv()

            @pl.when(jnp.logical_not(top))
            def _():
                down_copy().wait_recv()

        low = jnp.where(i <= 1, 0, 2 * i)
        high = jnp.where(i == 0, 0, jnp.where(i == pairs - 1, planes + 2, 2 * i + 2))
        lax.fori_loop(low, high, first, 0)

        @pl.when(i == 1)
        def _():
            @pl.when(bottom)
            def _():
                fill(mid, 0, 1, (1.0, solid_u))

            @pl.when(top)
            def _():
                fill(mid, planes + 1, 1, (-1.0, liquid_u))

        low = jnp.maximum(i - 2, 0)
        high = jnp.where(i == pairs - 1, pairs, jnp.maximum(i - 1, 0))
        lax.fori_loop(low, high, second, 0)

        @pl.when(bottom & ((i == planes // 4 + 1) | (i == pairs - 1)))
        def _():
            coarsen(jnp.where(i == pairs - 1, 1, 0))
        return carry

    lax.fori_loop(0, pairs, turn, 0)

    def finish(k, carry):
        for copy in sides(k):
            copy.wait_send()

        @pl.when(grow > 0)
        def _():
            for copy in out_copies(k):
                copy.wait_send()

        @pl.when(jnp.logical_not(top))
        def _():
            for copy in out_copies(k):
                copy.wait_recv()
        return carry

    lax.fori_loop(0, pairs, finish, 0)

    @pl.when(top)
    def _():
        for copy in blanks():
            copy.wait()

    @pl.when(jnp.logical_not(top))
    def _():
        up_copy().wait_send()

    @pl.when(grow > 0)
    def _():
        down_copy().wait_send()

    def others(half):
        return landed.at[half, pl.ds(0, lat_count - 1)]

    @pl.when(bottom)
    def _():
        for half in range(2):
            pltpu.make_async_copy(others(half), others(half), piece_recv.at[half]).wait()

    @pl.when(grow > 0)
    def _():
        for half in range(2):
            pltpu.make_async_copy(landed.at[half], landed.at[half], piece_recv.at[half]).wait()

    def find(k, found):
        return jnp.where(writer[grow, k] == lat, k, found)

    origin = lax.fori_loop(0, lat_count, find, 0)
    for half in range(2):
        mine = landed[half, origin]
        for f in range(2):
            for group in range(groups):
                at = f * groups + group
                check_out[0, 0, f, half * groups + group] = mine[at : at + 1, 0 : check_out.shape[5]]

    @pl.when(bottom)
    def _():
        for half in range(2):
            pltpu.make_async_copy(others(half), others(half), piece_send.at[half, 0]).wait()
            for r in range(1, grow_count):
                pltpu.make_async_copy(landed.at[half], landed.at[half], piece_send.at[half, r]).wait()


def store(phase, solute, check, phase_out, solute_out, check_out, sems, last):
    count = sems.shape[1]
    size = phase.shape[0] // count
    copies = [pltpu.make_async_copy(check, check_out, last)]
    for k in range(count):
        part = pl.ds(k * size, size)
        copies.append(pltpu.make_async_copy(phase.at[part], phase_out.at[part], sems.at[0, k]))
        copies.append(pltpu.make_async_copy(solute.at[part], solute_out.at[part], sems.at[1, k]))
    for copy in copies:
        copy.start()
    for copy in copies:
        copy.wait()


def shards(phase, solute, seed_grain, writer):
    planes, rows, width = phase.shape
    lat_count = lax.axis_size("lat")
    grow_count = lax.axis_size("grow")
    piece = width // 4 // grow_count
    lanes = -(-piece // 128) * 128
    wide = rows + 4
    pairs = planes // 2
    f32 = jnp.float32
    dma = pltpu.SemaphoreType.DMA
    vmem = pl.BlockSpec(memory_space=pltpu.VMEM)
    anywhere = pl.BlockSpec(memory_space=pltpu.HBM)
    results = pl.pallas_call(
        functools.partial(kernel, lat_count, grow_count),
        out_shape=(
            pltpu.VMEM(phase.shape, f32),
            pltpu.VMEM(phase.shape, f32),
            pltpu.VMEM((1, 1, 2, planes // 4, rows // 4, piece), f32),
        ),
        in_specs=[anywhere] * 4,
        out_specs=(vmem, vmem, vmem),
        scratch_shapes=[
            pltpu.VMEM((planes, 4, width), f32),
            pltpu.VMEM((planes, 4, width), f32),
            pltpu.VMEM((planes, 4, width), f32),
            pltpu.VMEM((planes, 4, width), f32),
            pltpu.VMEM((2, planes + 4, wide, width), f32),
            pltpu.VMEM((2, planes + 2, wide, width), f32),
            pltpu.VMEM((2, planes, rows, width), f32),
            pltpu.VMEM((2, grow_count, planes // 4, lanes), f32),
            pltpu.VMEM((2, lat_count, planes // 4, lanes), f32),
            dma((pairs,)), dma((pairs,)), dma((pairs,)), dma((pairs,)),
            dma((2,)), dma((2,)), dma((2, pairs)), dma((2, pairs)),
            dma((2, grow_count)), dma((2,)),
            pltpu.VMEM(phase.shape, f32),
            pltpu.VMEM(phase.shape, f32),
            dma((2, 4)),
            pltpu.VMEM(seed_grain.shape, jnp.int32),
            pltpu.SMEM(writer.shape, jnp.int32),
            dma((2,)),
            pltpu.VMEM((2, planes // 4, rows, width), f32),
            dma((2, 4)),
            pltpu.VMEM((width // grow_count, lanes), jnp.bfloat16),
        ],
        compiler_params=pltpu.CompilerParams(
            collective_id=0, has_side_effects=True, vmem_limit_bytes=vmem_bytes),
    )(phase, solute, seed_grain, writer)
    return tuple(pl.pallas_call(
        store,
        out_shape=tuple(jax.ShapeDtypeStruct(r.shape, f32) for r in results),
        in_specs=[vmem] * 3,
        out_specs=(anywhere,) * 3,
        scratch_shapes=[dma((2, 8)), dma],
        compiler_params=pltpu.CompilerParams(vmem_limit_bytes=8 * 1024 * 1024),
    )(*results))


def solution(mesh):
    placed = (P("grow", "lat", None), P("grow", "lat", None), P(), P())
    return jax.shard_map(
        shards,
        mesh=mesh,
        in_specs=placed,
        out_specs=(
            P("grow", "lat", None),
            P("grow", "lat", None),
            P("grow", "lat", None, None, None, None),
        ),
        check_vma=False,
    )
```
